32 devices in a mesh: row: 8 (over z, y), col: 4 (over x, core).
Axes of the slice: x: 2, y: 2, z: 4, core: 2. Of those that a mesh axis runs over, the one named last changes fastest.
Arguments:
- a11: float32 [256, 256], replicated, as said below
- linv11: float32 [256, 256], replicated, as said below
- a21: float32 [16384, 256], P(('row', 'col')), may hold values from -6 to 6
- l21: float32 [16384, 256], P(('row', 'col')), may hold values from -0.4 to 0.4
- a22: float32 [16384, 16384], P('row', 'col'), may hold values from -6 to 6
Outputs:
- diag_block: float32 [256, 256], replicated
- panel: float32 [16384, 256], P(('row', 'col'))
- trailing: float32 [16384, 16384], P('row', 'col')
The draws below stay inside these ranges and needn't reach their ends.
Inputs may be any that keep to these rules, and one draw needn't show every extreme that they name: `a11`: symmetric. `linv11`: lower triangular with a positive diagonal.
All inputs are finite; a program needn't handle non-finite values.
Results may differ from the reference program's by a relative error of at most 0.00005.
Values sent between devices are 32-bit elements; how exact they have to be, the bound alone decides.
No kernel may reach another device: no remote copies, remote signals or barrier semaphores. Data moves between devices by JAX's collectives and lax.ppermute only.
A program may use at most 128 MiB of HBM per device.

```python
import jax
import jax.numpy as jnp
from jax import lax

NB = 256
M = 16384


def draw_a11(key, part):
    gauss = jax.random.normal(key, (NB, NB), jnp.float32)
    return (gauss + gauss.T) * 0.5


def draw_linv11(key, part):
    first = jax.random.fold_in(key, 11)
    second = jax.random.fold_in(key, 12)
    diagonal = jax.random.uniform(first, (NB,), jnp.float32, 0.5, 1.0)
    lower = jax.random.normal(second, (NB, NB), jnp.float32) * (0.5 / NB ** 0.5)
    rows = jnp.arange(NB)[:, None]
    cols = jnp.arange(NB)[None, :]
    strict = jnp.where(rows > cols, lower, 0.0)
    return strict + jnp.diag(diagonal)


def shard_levels(own_key, dims, shards, low, largest):
    gain = 1.0
    for dim, parts in shards:
        steps = jax.random.uniform(jax.random.fold_in(jax.random.fold_in(own_key, 6), dim), (parts,), jnp.float32, low / len(shards), largest / len(shards))
        gain = gain * jnp.repeat(jnp.exp(steps), dims[dim] // parts).reshape((-1,) + (1,) * (len(dims) - 1 - dim))
    return gain


def normal_values(stream_key, extent, width, reach, split=(), kind=jnp.bfloat16):
    values = jax.random.normal(stream_key, extent, jnp.float32) * width
    if len(split) > 0:
        values = shard_levels(stream_key, extent, split, -0.22, 0.18) * values
    return jnp.clip(values, min=-reach, max=reach).astype(kind)


def setup_inputs(seed: int = 0) -> dict:
    key_of = jax.random.split(jax.random.key(seed), 6)
    return {
        "a11": draw_a11(jax.random.fold_in(key_of[5], 71), 0),
        "linv11": draw_linv11(jax.random.fold_in(key_of[5], 71), 0),
        "a21": normal_values(key_of[2], (M, NB), 1.0, 6.0, ((0, 32),), jnp.float32),
        "l21": normal_values(key_of[3], (M, NB), 0.0625, 0.4, ((0, 32),), jnp.float32),
        "a22": normal_values(key_of[4], (M, M), 1.0, 6.0, ((0, 8), (1, 4)), jnp.float32),
    }


def mult(a, b):
    return jnp.dot(a, b, precision=lax.Precision.HIGHEST, preferred_element_type=jnp.float32)


def reference(a11, linv11, a21, l21, a22):
    diag_block = mult(mult(linv11, a11), linv11.T)
    correction = 0.5 * mult(l21, diag_block)
    half = mult(a21, linv11.T) - correction
    trailing = a22 - (mult(half, l21.T) + mult(l21, half.T))
    panel = half - correction
    return diag_block, panel, trailing
```

```python
import functools

import jax
import jax.numpy as jnp
from jax import lax
from jax.experimental import pallas as pl
from jax.experimental.pallas import tpu as pltpu
from jax.sharding import PartitionSpec as P

AXES = ("row", "col")
MIB = 1 << 20
LAG = 1
KLAG = 0


def mult(a, b):
    return jnp.dot(a, b, precision=lax.Precision.HIGHEST, preferred_element_type=jnp.float32)


def dot_t(a, b, precision=None):
    return lax.dot_general(a, b, (((1,), (1,)), ((), ())), precision=precision, preferred_element_type=jnp.float32)


def split(x):
    hi = x.astype(jnp.bfloat16)
    lo = (x - hi.astype(jnp.float32)).astype(jnp.bfloat16)
    return hi, lo


def front_kernel(a11_ref, linv_ref, a21_ref, l21_ref, diag_ref, panel_ref, *piece_refs):
    high = lax.Precision.HIGHEST
    linv = linv_ref[...]
    width = linv.shape[0]
    diag = dot_t(mult(linv, a11_ref[...]), linv, high)
    diag_ref[...] = diag
    rows = piece_refs[0].shape[0]
    for q, piece in enumerate(piece_refs):
        low = l21_ref[pl.ds(q * rows, rows), :]
        correction = 0.5 * mult(low, diag)
        half = dot_t(a21_ref[pl.ds(q * rows, rows), :], linv, high) - correction
        panel_ref[pl.ds(q * rows, rows), :] = half - correction
        piece[:, :width] = low
        piece[:, width:] = half


def rows_kernel(parts, me_ref, *refs):
    pieces, (hi_ref, lo_ref) = refs[:-2], refs[-2:]
    rows, both = pieces[0].shape
    width = both // 2
    for p, piece in enumerate(pieces):
        i, q = divmod(p, parts)
        at = pl.multiple_of(((me_ref[0] ^ i) * parts + q) * rows, rows)
        for dst, src in ((0, width), (width, 0)):
            hi, lo = split(piece[:, src : src + width])
            hi_ref[pl.ds(at, rows), dst : dst + width] = hi
            lo_ref[pl.ds(at, rows), dst : dst + width] = lo


def update_kernel(step, n_piece, block, table_ref, hi_ref, lo_ref, *refs):
    pieces = refs[:n_piece]
    scratch = refs[len(refs) - 2 * n_piece :]
    old_ref, new_ref = refs[n_piece], refs[len(refs) - 2 * n_piece - 1]
    rows, both = pieces[0].shape

    @pl.when(table_ref[step, 0] != 0)
    def _():
        for k, piece in enumerate(pieces):
            hi, lo = split(piece[...])
            scratch[2 * k][...] = hi
            scratch[2 * k + 1][...] = lo

        def body(a_hi, a_lo, *tiles):
            for k in range(n_piece):
                b_hi, b_lo = scratch[2 * k][...], scratch[2 * k + 1][...]
                left, low = a_hi[...], a_lo[...]
                total = dot_t(left, b_hi) + (dot_t(left, b_lo) + dot_t(low, b_hi))
                tiles[n_piece + k][...] = tiles[k][...] - total

        tile = [
            pl.BlockSpec((block, rows), lambda i, k=k: (i, table_ref[step, 1 + k]))
            for k in range(n_piece)
        ]
        operand = pl.BlockSpec((block, both), lambda i: (i, 0))
        pltpu.emit_pipeline(
            body,
            grid=(old_ref.shape[0] // block,),
            in_specs=[operand, operand] + tile,
            out_specs=tile,
        )(hi_ref, lo_ref, *([old_ref] * n_piece), *([new_ref] * n_piece))


def update(step, table, a_hi, a_lo, pieces, old, new):
    rows, both = pieces[0].shape
    n = len(pieces)
    height, columns = old.shape
    block = min(512, height)
    whole = pl.BlockSpec(memory_space=pl.ANY)
    held = pl.BlockSpec(memory_space=pltpu.VMEM)
    first = new is None
    return pl.pallas_call(
        functools.partial(update_kernel, step, n, block),
        grid_spec=pltpu.PrefetchScalarGridSpec(
            num_scalar_prefetch=1,
            grid=(),
            in_specs=[whole, whole] + [held] * n + [whole] * (1 if first else 2),
            out_specs=whole,
            scratch_shapes=[pltpu.VMEM((rows, both), jnp.bfloat16)] * (2 * n),
        ),
        out_shape=jax.ShapeDtypeStruct(old.shape, old.dtype),
        input_output_aliases={} if first else {3 + n + 1: 0},
        compiler_params=pltpu.CompilerParams(vmem_limit_bytes=24 * MIB),
        cost_estimate=pl.CostEstimate(
            flops=6 * n * height * rows * both,
            bytes_accessed=8 * n * height * rows + 4 * height * both,
            transcendentals=0,
        ),
        name="update",
    )(table, a_hi, a_lo, *pieces, old, *([] if first else [new]))


def place_pieces(across, line, pieces):
    for k, piece in enumerate(pieces):
        at = line[1 + k] * piece.shape[0]
        kept = lax.dynamic_slice_in_dim(across, at, piece.shape[0], 0)
        across = lax.dynamic_update_slice_in_dim(across, jnp.where(line[0] != 0, piece, kept), at, 0)
    return across


def solution(mesh):
    n_row, n_col = mesh.shape["row"], mesh.shape["col"]
    groups = n_row // n_col
    chain = n_col

    def at(place, g, c):
        return (place * groups + g) * n_col + c

    everyone = [(place, g, c) for place in range(chain) for g in range(groups) for c in range(n_col)]

    def sign(c):
        return 1 if c < n_col // 2 else -1

    def ahead(place, c):
        return (place + sign(c)) % chain

    ring = [(at(p, g, c), at(ahead(p, c), g, c)) for p, g, c in everyone]

    def swap_group(bit):
        return [(at(p, g, c), at(p, g ^ bit, c)) for p, g, c in everyone]

    def swap_col(bit):
        return [(at(p, g, c), at(p, g, c ^ bit)) for p, g, c in everyone]

    def send(value, pairs):
        return lax.ppermute(value, AXES, pairs)

    def body(a11, linv11, a21, l21, a22):
        rows, width = l21.shape
        parts = 2 if rows % 256 == 0 else 1
        r, c = lax.axis_index("row"), lax.axis_index("col")
        place, g = r // groups, r % groups
        far = jnp.where(c < n_col // 2, place - c, c - place) % chain

        piece = jax.ShapeDtypeStruct((rows // parts, 2 * width), jnp.float32)
        diag_block, panel, *own = pl.pallas_call(
            front_kernel,
            out_shape=[
                jax.ShapeDtypeStruct(a11.shape, jnp.float32),
                jax.ShapeDtypeStruct(a21.shape, jnp.float32),
            ]
            + [piece] * parts,
            compiler_params=pltpu.CompilerParams(vmem_limit_bytes=24 * MIB),
            name="front",
        )(a11, linv11, a21, l21)

        held = {0: own}
        bit = n_col // 2
        while bit:
            for i in sorted(held):
                held[i | bit] = [send(v, swap_col(bit)) for v in held[i]]
            bit //= 2
        source = [v for i in range(n_col) for v in held[i]]

        wide = rows // parts % 128 == 0
        a_hi, a_lo = pl.pallas_call(
            functools.partial(rows_kernel, parts),
            in_specs=[pl.BlockSpec(memory_space=pltpu.SMEM)] + [pl.BlockSpec(memory_space=pltpu.VMEM)] * len(source),
            out_shape=[jax.ShapeDtypeStruct((n_col * rows, 2 * width), jnp.bfloat16)] * 2,
            compiler_params=pltpu.CompilerParams(vmem_limit_bytes=32 * MIB),
            name="rows",
        )(c.astype(jnp.int32)[None], *source)

        count = len(source)
        steps = count + chain - 1
        index = jnp.arange(steps, dtype=jnp.int32) - far
        good = (index >= 0) & (index < count)
        index = jnp.clip(index, 0, count - 1)
        column = (c ^ (index // parts)) * parts + index % parts
        table = jnp.stack(
            [good.astype(jnp.int32)] + [(g ^ other) * n_col * parts + column for other in range(groups)], axis=1
        ).astype(jnp.int32)

        trailing = None
        across = jnp.zeros((a22.shape[1], 2 * width), jnp.float32)
        current = source[0]
        others = []
        states = []
        for t in range(steps):
            others.append([send(current, swap_group(b)) for b in range(1, groups)])
            if wide:
                trailing = update(t, table, a_hi, a_lo, [current] + others[t], a22, trailing)
            else:
                across = place_pieces(across, table[t], [current] + others[t])
            states.append(trailing)
            if t + 1 < steps:
                following = send(current, ring)
                if t >= LAG:
                    following, others[t - LAG] = lax.optimization_barrier((following, others[t - LAG]))
                current = jnp.where(far == 0, source[t + 1], following) if t + 1 < count else following
        if not wide:
            left = a_hi.astype(jnp.float32) + a_lo.astype(jnp.float32)
            trailing = a22 - dot_t(left, across, lax.Precision.HIGHEST)
        return diag_block, panel, trailing

    return jax.shard_map(
        body,
        mesh=mesh,
        in_specs=(P(), P(), P(AXES, None), P(AXES, None), P("row", "col")),
        out_specs=(P(), P(AXES, None), P("row", "col")),
        check_vma=False,
    )
```

```python
import functools

import jax
import jax.numpy as jnp
from jax import lax
from jax.experimental import pallas as pl
from jax.experimental.pallas import tpu as pltpu
from jax.sharding import PartitionSpec as P

AXES = ("row", "col")
MIB = 1 << 20
LATE = 2
YEARLY = 2
CLOSED = 4


def mult(a, b, precision=lax.Precision.HIGHEST):
    return jnp.dot(a, b, precision=precision, preferred_element_type=jnp.float32)


def mult_t(a, b, precision=lax.Precision.HIGHEST):
    return lax.dot_general(a, b, (((1,), (1,)), ((), ())), precision=precision, preferred_element_type=jnp.float32)


def split(x):
    hi = x.astype(jnp.bfloat16)
    lo = (x - hi.astype(jnp.float32)).astype(jnp.bfloat16)
    return hi, lo


def front_kernel(parts, *refs):
    arrays, outs, scratch = refs[:4], refs[4 : 6 + parts], refs[6 + parts :]
    diag_ref, panel_ref, *piece_refs = outs
    a11_ref, linv_ref, a21_ref, l21_ref, came = scratch
    copies = []
    for k, (src, dst) in enumerate(zip(arrays, scratch)):
        rows = src.shape[0] // 2
        for half in range(2):
            here = pl.ds(half * rows, rows)
            copies.append(pltpu.make_async_copy(src.at[here], dst.at[here], came.at[2 * k + half]))
    for copy in copies:
        copy.start()
    for copy in copies[:4]:
        copy.wait()
    linv = linv_ref[...]
    width = linv.shape[0]
    diag = mult_t(mult(linv, a11_ref[...]), linv)
    diag_ref[...] = diag
    for copy in copies[4:]:
        copy.wait()
    rows = piece_refs[0].shape[0]
    for q, piece in enumerate(piece_refs):
        low = l21_ref[pl.ds(q * rows, rows), :]
        correction = 0.5 * mult(low, diag)
        half = mult_t(a21_ref[pl.ds(q * rows, rows), :], linv) - correction
        panel_ref[pl.ds(q * rows, rows), :] = half - correction
        piece[:, :width] = low
        piece[:, width:] = half


def fetch(pieces, scratch, came):
    copies = [pltpu.make_async_copy(piece, scratch.at[k], came.at[k]) for k, piece in enumerate(pieces)]
    for copy in copies:
        copy.start()
    return copies


def rows_kernel(*refs):
    pieces, (hi_ref, lo_ref, held, came) = refs[:-4], refs[-4:]
    rows, both = pieces[0].shape
    width = both // 2
    for q, copy in enumerate(fetch(pieces, held, came)):
        copy.wait()
        for dst, src in ((0, width), (width, 0)):
            hi, lo = split(held[q, :, src : src + width])
            hi_ref[q * rows : (q + 1) * rows, dst : dst + width] = hi
            lo_ref[q * rows : (q + 1) * rows, dst : dst + width] = lo


def rows_of(pieces):
    rows, both = pieces[0].shape
    n = len(pieces)
    shape = jax.ShapeDtypeStruct((n * rows, both), jnp.bfloat16)
    return pl.pallas_call(
        rows_kernel,
        in_specs=[pl.BlockSpec(memory_space=pl.ANY)] * n,
        scratch_shapes=[pltpu.VMEM((n, rows, both), jnp.float32), pltpu.SemaphoreType.DMA((n,))],
        out_shape=[shape, shape],
        compiler_params=pltpu.CompilerParams(vmem_limit_bytes=36 * MIB),
        name="rows",
    )(*pieces)


def update_kernel(chunks, items, cases, table_ref, *refs):
    left, refs = refs[: 2 * chunks], refs[2 * chunks :]
    pieces, old_ref = refs[: len(items)], refs[len(items)]
    new_ref, held, tile, b_hi, b_lo, got, came, went = refs[-8:]
    rows = pieces[0].shape[0]
    height = left[0].shape[0]
    bands = [(i, 0, height) for i in range(chunks - 1)]
    bands += [(chunks - 1, s * height // 2, height // 2) for s in range(2)]

    def place(b, k):
        i, start, size = bands[b]
        step, column = items[k]
        down = (table_ref[step, 1] ^ i) * height + start
        across = pl.multiple_of(table_ref[step, 2 + column] * rows, rows)
        return pl.ds(pl.multiple_of(down, size), size), pl.ds(across, rows)

    def inner(b, k):
        i, start, size = bands[b]
        return tile.at[k, pl.ds(i * height + start, size)]

    def read(b, k):
        return pltpu.make_async_copy(old_ref.at[place(b, k)], inner(b, k), came.at[k, b])

    def write(b, k):
        return pltpu.make_async_copy(inner(b, k), new_ref.at[place(b, k)], went.at[k, b])

    def run(n):
        for b in range(len(bands)):
            for k in range(n):
                if b == 0 and k == 0:
                    copies = fetch(pieces[:n], held, got)
                read(b, k).start()
        for k, copy in enumerate(copies):
            copy.wait()
            hi, lo = split(held[k])
            b_hi[:, k * rows : (k + 1) * rows] = hi.T
            b_lo[:, k * rows : (k + 1) * rows] = lo.T
        for b, (i, start, size) in enumerate(bands):
            a_hi = left[2 * i][start : start + size, :]
            a_lo = left[2 * i + 1][start : start + size, :]
            right, low = b_hi[:, : n * rows], b_lo[:, : n * rows]
            total = mult(a_hi, right, None) + (mult(a_hi, low, None) + mult(a_lo, right, None))
            for k in range(n):
                read(b, k).wait()
            here = pl.ds(i * height + start, size)
            for k in range(n):
                tile[k, here] = tile[k, here] - total[:, k * rows : (k + 1) * rows]
            for k in range(n):
                write(b, k).start()
        for b in range(len(bands)):
            for k in range(n):
                write(b, k).wait()

    for n, wanted, barred in cases:
        due = table_ref[wanted, 0] != 0
        if barred is not None:
            due = due & (table_ref[barred, 0] == 0)
        pl.when(due)(functools.partial(run, n))


def update(table, left, items, cases, pieces, old, new):
    rows, both = pieces[0].shape
    n, chunks = len(pieces), len(left) // 2
    height = old.shape[0]
    whole = pl.BlockSpec(memory_space=pl.ANY)
    held = pl.BlockSpec(memory_space=pltpu.VMEM)
    first = new is None
    before = 1 + len(left) + n
    return pl.pallas_call(
        functools.partial(update_kernel, chunks, items, cases),
        grid_spec=pltpu.PrefetchScalarGridSpec(
            num_scalar_prefetch=1,
            grid=(),
            in_specs=[held] * len(left) + [whole] * (n + (1 if first else 2)),
            out_specs=whole,
            scratch_shapes=[
                pltpu.VMEM((n, rows, both), jnp.float32),
                pltpu.VMEM((n, height, rows), jnp.float32),
                pltpu.VMEM((both, n * rows), jnp.bfloat16),
                pltpu.VMEM((both, n * rows), jnp.bfloat16),
                pltpu.SemaphoreType.DMA((n,)),
                pltpu.SemaphoreType.DMA((n, chunks + 1)),
                pltpu.SemaphoreType.DMA((n, chunks + 1)),
            ],
        ),
        out_shape=jax.ShapeDtypeStruct(old.shape, old.dtype),
        input_output_aliases={} if first else {before + 1: 0},
        compiler_params=pltpu.CompilerParams(vmem_limit_bytes=36 * MIB),
        cost_estimate=pl.CostEstimate(
            flops=6 * n * height * rows * both,
            bytes_accessed=8 * n * height * rows,
            transcendentals=0,
        ),
        name="update",
    )(table, *left, *pieces, old, *([] if first else [new]))


def place_pieces(across, line, pieces):
    for k, piece in enumerate(pieces):
        at = line[2 + k] * piece.shape[0]
        kept = lax.dynamic_slice_in_dim(across, at, piece.shape[0], 0)
        across = lax.dynamic_update_slice_in_dim(across, jnp.where(line[0] != 0, piece, kept), at, 0)
    return across


def solution(mesh):
    n_row, n_col = mesh.shape["row"], mesh.shape["col"]
    groups = n_row // n_col
    chain = n_col

    def at(place, g, c):
        return (place * groups + g) * n_col + c

    everyone = [(place, g, c) for place in range(chain) for g in range(groups) for c in range(n_col)]

    def ahead(place, c):
        return (place + (1 if c < n_col // 2 else -1)) % chain

    def far_of(place, c):
        return (place - c if c < n_col // 2 else c - place) % chain

    def onward(place, g, c):
        if far_of(place, c) < chain - 1:
            return at(ahead(place, c), g, c)
        return at(c ^ 1, g, c ^ 1)

    def ring(t, count):
        return [
            (at(p, g, c), onward(p, g, c))
            for p, g, c in everyone
            if t < CLOSED or (far_of(p, c) < chain - 1 and t - far_of(p, c) < count)
        ]

    def swap_group(bit):
        return [(at(p, g, c), at(p, g ^ bit, c)) for p, g, c in everyone]

    def swap_col(bit):
        return [(at(p, g, c), at(p, g, c ^ bit)) for p, g, c in everyone]

    def send(value, pairs):
        return lax.ppermute(value, AXES, pairs)

    def body(a11, linv11, a21, l21, a22):
        rows, width = l21.shape
        parts = 2 if rows % 256 == 0 else 1
        r, c = lax.axis_index("row"), lax.axis_index("col")
        place, g = r // groups, r % groups
        far = jnp.where(c < n_col // 2, place - c, c - place) % chain
        wide = rows // parts % 128 == 0

        piece = jax.ShapeDtypeStruct((rows // parts, 2 * width), jnp.float32)
        diag_block, panel, *own = pl.pallas_call(
            functools.partial(front_kernel, parts),
            in_specs=[pl.BlockSpec(memory_space=pl.ANY)] * 4,
            scratch_shapes=[pltpu.VMEM(v.shape, jnp.float32) for v in (a11, linv11, a21, l21)]
            + [pltpu.SemaphoreType.DMA((8,))],
            out_shape=[
                jax.ShapeDtypeStruct(a11.shape, jnp.float32),
                jax.ShapeDtypeStruct(a21.shape, jnp.float32),
            ]
            + [piece] * parts,
            compiler_params=pltpu.CompilerParams(vmem_limit_bytes=60 * MIB),
            name="front",
        )(a11, linv11, a21, l21)

        held = {0: own}
        bit = n_col // 2
        while bit:
            for i in sorted(held):
                held[i | bit] = [send(v, swap_col(bit)) for v in held[i]]
            bit //= 2

        left = []
        if wide:
            left = [part for i in range(n_col) for part in rows_of(held[i])]
        source = [v for i in range(n_col) for v in held[i]]

        count = len(source)
        steps = count + chain - 1
        index = jnp.arange(steps, dtype=jnp.int32) - far
        good = (index >= 0) & (index < count)
        index = jnp.clip(index, 0, count - 1)
        column = (c ^ (index // parts)) * parts + index % parts
        table = jnp.stack(
            [good.astype(jnp.int32), jnp.broadcast_to(c, (steps,))]
            + [(g ^ other) * n_col * parts + column for other in range(groups)],
            axis=1,
        ).astype(jnp.int32)

        trailing = None
        across = jnp.zeros((a22.shape[1], 2 * width), jnp.float32)
        current = source[0]
        currents, others = [], []
        late = min(LATE, steps - 1)
        after = {t + 1: [t] for t in range(late, steps - 1)}
        for u in range(late):
            after.setdefault(steps - late + u, []).insert(0, u)

        def arrived(u):
            return [currents[u]] + others[u]

        for t in range(steps):
            currents.append(current)
            if t + 1 < steps:
                following = send(current, ring(t, count))
            others.append([send(current, swap_group(b)) for b in range(1, groups)])
            for u in after.get(t, []):
                if not wide:
                    across = place_pieces(across, table[u], arrived(u))
                    continue
                pieces = arrived(u)
                items = [(u, k) for k in range(groups)]
                cases = [(groups, u, None)]
                if u == steps - 2:
                    trailing = update(table, left, [(u + 1, 0)], [(1, u + 1, None)], [current], a22, trailing)
                trailing = update(table, left, items, cases, pieces, a22, trailing)
            if t + 1 < steps:
                if t == 2:
                    following, source, left = lax.optimization_barrier((following, source, left))
                if t <= YEARLY:
                    following, others[t], trailing = lax.optimization_barrier((following, others[t], trailing))
                else:
                    following, trailing = lax.optimization_barrier((following, trailing))
                current = jnp.where(far == 0, source[t + 1], following) if t + 1 < count else following
        if wide:
            for k, piece in enumerate(others[-1]):
                trailing = update(table, left, [(steps - 1, 1 + k)], [(1, steps - 1, None)], [piece], a22, trailing)
        else:
            across = place_pieces(across, table[steps - 1], [currents[-1]] + others[-1])
            mine = jnp.zeros((n_col * rows, 2 * width), jnp.float32)
            for i in range(n_col):
                chunk = jnp.roll(jnp.concatenate(held[i], axis=0), width, axis=1)
                mine = lax.dynamic_update_slice_in_dim(mine, chunk, (c ^ i) * rows, 0)
            trailing = a22 - mult_t(mine, across)
        return diag_block, panel, trailing

    return jax.shard_map(
        body,
        mesh=mesh,
        in_specs=(P(), P(), P(AXES, None), P(AXES, None), P("row", "col")),
        out_specs=(P(), P(AXES, None), P("row", "col")),
        check_vma=False,
    )
```

```python
import functools

import jax
import jax.numpy as jnp
from jax import lax
from jax.experimental import pallas as pl
from jax.experimental.pallas import tpu as pltpu
from jax.sharding import PartitionSpec as P

AXES = ("row", "col")
MIB = 1 << 20
LATE = 2
YEARLY = 1
CLOSED = 4


def mult(a, b, precision=lax.Precision.HIGHEST):
    return jnp.dot(a, b, precision=precision, preferred_element_type=jnp.float32)


def mult_t(a, b, precision=lax.Precision.HIGHEST):
    return lax.dot_general(a, b, (((1,), (1,)), ((), ())), precision=precision, preferred_element_type=jnp.float32)


def split(x):
    hi = x.astype(jnp.bfloat16)
    lo = (x - hi.astype(jnp.float32)).astype(jnp.bfloat16)
    return hi, lo


def front_kernel(parts, *refs):
    arrays, outs, scratch = refs[:4], refs[4 : 6 + parts], refs[6 + parts :]
    diag_ref, panel_ref, *piece_refs = outs
    a11_ref, linv_ref, a21_ref, l21_ref, came = scratch
    copies = []
    for k, (src, dst) in enumerate(zip(arrays, scratch)):
        rows = src.shape[0] // 2
        for half in range(2):
            here = pl.ds(half * rows, rows)
            copies.append(pltpu.make_async_copy(src.at[here], dst.at[here], came.at[2 * k + half]))
    for copy in copies:
        copy.start()
    for copy in copies[:4]:
        copy.wait()
    linv = linv_ref[...]
    width = linv.shape[0]
    diag = mult_t(mult(linv, a11_ref[...]), linv)
    diag_ref[...] = diag
    for copy in copies[4:]:
        copy.wait()
    rows = piece_refs[0].shape[0]
    for q, piece in enumerate(piece_refs):
        low = l21_ref[pl.ds(q * rows, rows), :]
        correction = 0.5 * mult(low, diag)
        half = mult_t(a21_ref[pl.ds(q * rows, rows), :], linv) - correction
        panel_ref[pl.ds(q * rows, rows), :] = half - correction
        piece[:, :width] = low
        piece[:, width:] = half


def fetch(pieces, scratch, came):
    copies = [pltpu.make_async_copy(piece, scratch.at[k], came.at[k]) for k, piece in enumerate(pieces)]
    for copy in copies:
        copy.start()
    return copies


def rows_kernel(*refs):
    pieces, (hi_ref, lo_ref, held, came) = refs[:-4], refs[-4:]
    rows, both = pieces[0].shape
    width = both // 2
    for q, copy in enumerate(fetch(pieces, held, came)):
        copy.wait()
        for dst, src in ((0, width), (width, 0)):
            hi, lo = split(held[q, :, src : src + width])
            hi_ref[q * rows : (q + 1) * rows, dst : dst + width] = hi
            lo_ref[q * rows : (q + 1) * rows, dst : dst + width] = lo


def rows_of(pieces):
    rows, both = pieces[0].shape
    n = len(pieces)
    shape = jax.ShapeDtypeStruct((n * rows, both), jnp.bfloat16)
    return pl.pallas_call(
        rows_kernel,
        in_specs=[pl.BlockSpec(memory_space=pl.ANY)] * n,
        scratch_shapes=[pltpu.VMEM((n, rows, both), jnp.float32), pltpu.SemaphoreType.DMA((n,))],
        out_shape=[shape, shape],
        compiler_params=pltpu.CompilerParams(vmem_limit_bytes=36 * MIB),
        name="rows",
    )(*pieces)


def update_kernel(chunks, items, cases, table_ref, *refs):
    left, refs = refs[: 2 * chunks], refs[2 * chunks :]
    pieces, old_ref = refs[: len(items)], refs[len(items)]
    new_ref, held, tile, b_hi, b_lo, got, came, went = refs[-8:]
    rows = pieces[0].shape[0]
    height = left[0].shape[0]
    bands = [(i, 0, height) for i in range(chunks - 1)]
    bands += [(chunks - 1, s * height // 2, height // 2) for s in range(2)]

    def place(b, k):
        i, start, size = bands[b]
        step, column = items[k]
        down = (table_ref[step, 1] ^ i) * height + start
        across = pl.multiple_of(table_ref[step, 2 + column] * rows, rows)
        return pl.ds(pl.multiple_of(down, size), size), pl.ds(across, rows)

    def inner(b, k):
        i, start, size = bands[b]
        return tile.at[k, pl.ds(i * height + start, size)]

    def read(b, k):
        return pltpu.make_async_copy(old_ref.at[place(b, k)], inner(b, k), came.at[k, b])

    def write(b, k):
        return pltpu.make_async_copy(inner(b, k), new_ref.at[place(b, k)], went.at[k, b])

    def run(n):
        for b in range(len(bands)):
            for k in range(n):
                if b == 0 and k == 0:
                    copies = fetch(pieces[:n], held, got)
                read(b, k).start()
        for k, copy in enumerate(copies):
            copy.wait()
            hi, lo = split(held[k])
            b_hi[:, k * rows : (k + 1) * rows] = hi.T
            b_lo[:, k * rows : (k + 1) * rows] = lo.T
        for b, (i, start, size) in enumerate(bands):
            a_hi = left[2 * i][start : start + size, :]
            a_lo = left[2 * i + 1][start : start + size, :]
            right, low = b_hi[:, : n * rows], b_lo[:, : n * rows]
            total = mult(a_hi, right, None) + (mult(a_hi, low, None) + mult(a_lo, right, None))
            for k in range(n):
                read(b, k).wait()
            here = pl.ds(i * height + start, size)
            for k in range(n):
                tile[k, here] = tile[k, here] - total[:, k * rows : (k + 1) * rows]
            for k in range(n):
                write(b, k).start()
        for b in range(len(bands)):
            for k in range(n):
                write(b, k).wait()

    for n, wanted, barred in cases:
        due = table_ref[wanted, 0] != 0
        if barred is not None:
            due = due & (table_ref[barred, 0] == 0)
        pl.when(due)(functools.partial(run, n))


def update(table, left, items, cases, pieces, old, new):
    rows, both = pieces[0].shape
    n, chunks = len(pieces), len(left) // 2
    height = old.shape[0]
    whole = pl.BlockSpec(memory_space=pl.ANY)
    held = pl.BlockSpec(memory_space=pltpu.VMEM)
    first = new is None
    before = 1 + len(left) + n
    return pl.pallas_call(
        functools.partial(update_kernel, chunks, items, cases),
        grid_spec=pltpu.PrefetchScalarGridSpec(
            num_scalar_prefetch=1,
            grid=(),
            in_specs=[held] * len(left) + [whole] * (n + (1 if first else 2)),
            out_specs=whole,
            scratch_shapes=[
                pltpu.VMEM((n, rows, both), jnp.float32),
                pltpu.VMEM((n, height, rows), jnp.float32),
                pltpu.VMEM((both, n * rows), jnp.bfloat16),
                pltpu.VMEM((both, n * rows), jnp.bfloat16),
                pltpu.SemaphoreType.DMA((n,)),
                pltpu.SemaphoreType.DMA((n, chunks + 1)),
                pltpu.SemaphoreType.DMA((n, chunks + 1)),
            ],
        ),
        out_shape=jax.ShapeDtypeStruct(old.shape, old.dtype),
        input_output_aliases={} if first else {before + 1: 0},
        compiler_params=pltpu.CompilerParams(vmem_limit_bytes=36 * MIB),
        cost_estimate=pl.CostEstimate(
            flops=6 * n * height * rows * both,
            bytes_accessed=8 * n * height * rows,
            transcendentals=0,
        ),
        name="update",
    )(table, *left, *pieces, old, *([] if first else [new]))


def place_pieces(across, line, pieces):
    for k, piece in enumerate(pieces):
        at = line[2 + k] * piece.shape[0]
        kept = lax.dynamic_slice_in_dim(across, at, piece.shape[0], 0)
        across = lax.dynamic_update_slice_in_dim(across, jnp.where(line[0] != 0, piece, kept), at, 0)
    return across


def solution(mesh):
    n_row, n_col = mesh.shape["row"], mesh.shape["col"]
    groups = n_row // n_col
    chain = n_col

    def at(place, g, c):
        return (place * groups + g) * n_col + c

    everyone = [(place, g, c) for place in range(chain) for g in range(groups) for c in range(n_col)]

    def ahead(place, c):
        return (place + (1 if c < n_col // 2 else -1)) % chain

    def far_of(place, c):
        return (place - c if c < n_col // 2 else c - place) % chain

    def onward(place, g, c):
        if far_of(place, c) < chain - 1:
            return at(ahead(place, c), g, c)
        return at(c ^ 1, g, c ^ 1)

    def ring(t, count):
        return [
            (at(p, g, c), onward(p, g, c))
            for p, g, c in everyone
            if t < CLOSED or (far_of(p, c) < chain - 1 and t - far_of(p, c) < count)
        ]

    def swap_group(bit):
        return [(at(p, g, c), at(p, g ^ bit, c)) for p, g, c in everyone]

    def swap_col(bit):
        return [(at(p, g, c), at(p, g, c ^ bit)) for p, g, c in everyone]

    def send(value, pairs):
        return lax.ppermute(value, AXES, pairs)

    def body(a11, linv11, a21, l21, a22):
        rows, width = l21.shape
        parts = 2 if rows % 256 == 0 else 1
        r, c = lax.axis_index("row"), lax.axis_index("col")
        place, g = r // groups, r % groups
        far = jnp.where(c < n_col // 2, place - c, c - place) % chain
        wide = rows // parts % 128 == 0

        piece = jax.ShapeDtypeStruct((rows // parts, 2 * width), jnp.float32)
        diag_block, panel, *own = pl.pallas_call(
            functools.partial(front_kernel, parts),
            in_specs=[pl.BlockSpec(memory_space=pl.ANY)] * 4,
            scratch_shapes=[pltpu.VMEM(v.shape, jnp.float32) for v in (a11, linv11, a21, l21)]
            + [pltpu.SemaphoreType.DMA((8,))],
            out_shape=[
                jax.ShapeDtypeStruct(a11.shape, jnp.float32),
                jax.ShapeDtypeStruct(a21.shape, jnp.float32),
            ]
            + [piece] * parts,
            compiler_params=pltpu.CompilerParams(vmem_limit_bytes=60 * MIB),
            name="front",
        )(a11, linv11, a21, l21)

        held = {0: own}
        bit = n_col // 2
        while bit:
            for i in sorted(held):
                held[i | bit] = [send(v, swap_col(bit)) for v in held[i]]
            bit //= 2

        left = []
        if wide:
            left = [part for i in range(n_col) for part in rows_of(held[i])]
        source = [v for i in range(n_col) for v in held[i]]

        count = len(source)
        steps = count + chain - 1
        index = jnp.arange(steps, dtype=jnp.int32) - far
        good = (index >= 0) & (index < count)
        index = jnp.clip(index, 0, count - 1)
        column = (c ^ (index // parts)) * parts + index % parts
        table = jnp.stack(
            [good.astype(jnp.int32), jnp.broadcast_to(c, (steps,))]
            + [(g ^ other) * n_col * parts + column for other in range(groups)],
            axis=1,
        ).astype(jnp.int32)

        trailing = None
        across = jnp.zeros((a22.shape[1], 2 * width), jnp.float32)
        current = source[0]
        currents, others = [], []
        late = min(LATE, steps - 1)
        after = {t + 1: [t] for t in range(late, steps - 1)}
        for u in range(late):
            after.setdefault(steps - late + u, []).insert(0, u)

        def arrived(u):
            return [currents[u]] + others[u]

        for t in range(steps):
            currents.append(current)
            if t + 1 < steps:
                following = send(current, ring(t, count))
            others.append([send(current, swap_group(b)) for b in range(1, groups)])
            for u in after.get(t, []):
                if not wide:
                    across = place_pieces(across, table[u], arrived(u))
                    continue
                pieces = arrived(u)
                items = [(u, k) for k in range(groups)]
                cases = [(groups, u, None)]
                if u == steps - 2:
                    trailing = update(table, left, [(u + 1, 0)], [(1, u + 1, None)], [current], a22, trailing)
                trailing = update(table, left, items, cases, pieces, a22, trailing)
            if t + 1 < steps:
                if t == 2:
                    following, source, left = lax.optimization_barrier((following, source, left))
                if t <= YEARLY:
                    following, others[t], trailing = lax.optimization_barrier((following, others[t], trailing))
                else:
                    following, trailing = lax.optimization_barrier((following, trailing))
                current = jnp.where(far == 0, source[t + 1], following) if t + 1 < count else following
        if wide:
            for k, piece in enumerate(others[-1]):
                trailing = update(table, left, [(steps - 1, 1 + k)], [(1, steps - 1, None)], [piece], a22, trailing)
        else:
            across = place_pieces(across, table[steps - 1], [currents[-1]] + others[-1])
            mine = jnp.zeros((n_col * rows, 2 * width), jnp.float32)
            for i in range(n_col):
                chunk = jnp.roll(jnp.concatenate(held[i], axis=0), width, axis=1)
                mine = lax.dynamic_update_slice_in_dim(mine, chunk, (c ^ i) * rows, 0)
            trailing = a22 - mult_t(mine, across)
        return diag_block, panel, trailing

    return jax.shard_map(
        body,
        mesh=mesh,
        in_specs=(P(), P(), P(AXES, None), P(AXES, None), P("row", "col")),
        out_specs=(P(), P(AXES, None), P("row", "col")),
        check_vma=False,
    )
```
